32 devices in a mesh: groups: 2 (over x), row: 16 (over z, y, core).
Axes of the slice: x: 2, y: 2, z: 4, core: 2. Of those that a mesh axis runs over, the one named last changes fastest.
Arguments:
- source_features: bfloat16 [32768, 64], P(('groups', 'row')), parts along dimension 0, may hold values from -80 to 80
- target_features: bfloat16 [262144, 64], P('groups'), parts along dimension 0, may hold values from -4 to 4
- source_weights: float32 [32768], P(('groups', 'row')), parts along dimension 0, may hold values from -1 to 1
- target_weights: float32 [262144], P('groups'), parts along dimension 0, may hold values from -1 to 1
- block_columns: int32 [128, 32], P(('groups', 'row')), parts along dimension 0, may hold values from 0 to 511, as said below
- block_counts: int32 [128], P(('groups', 'row')), parts along dimension 0, may hold values from 8 to 32
Outputs:
- source_potential: float32 [32768], P(('groups', 'row')), parts along dimension 0
- target_potential: float32 [262144], P(('groups', 'row')), parts along dimension 0
The draws below stay inside these ranges and needn't reach their ends.
There are 2 independent parts, one for each index of `groups`. The reference program is written for one: setup_inputs(seed, part) draws one part's arguments, and reference() takes and returns one part's arrays. A program takes and returns all parts, laid end to end along the dimension named above; each array names one. Nothing has to cross between parts.
Inputs may be any that keep to these rules, and one draw needn't show every extreme that they name: `block_columns`: the 32 entries of a row are distinct; every target block is named among the first block_counts[p] entries of some row p; entries from block_counts[p] on are not part of the support.
All inputs are finite; a program needn't handle non-finite values.
Results may differ from the reference program's by a relative error of at most 0.0003.
Values sent between devices are 32-bit elements; how exact they have to be, the bound alone decides.
A program may use at most 128 MiB of HBM per device.

```python
import jax
import jax.numpy as jnp
from jax import lax

FEAT = 64
BLOCK = 256
K = 32
ITERS = 3
BR_DEV = 4
TB = 512
SB = 64
NS = 16384
NT = 131072


def target_values(key):
    own_key = jax.random.fold_in(key, 41)
    values = 0.5 * jnp.clip(jax.random.normal(own_key, (NT, FEAT), jnp.float32), -8.0, 8.0)
    halves = values.reshape(NT // 2, 2, FEAT)
    second = halves[:, 1]
    halves = halves.at[:, 1].set(second)
    return halves.reshape(NT, FEAT)


def support(key):
    own_key = jax.random.fold_in(key, 51)
    reaching = (TB + SB - 1) // SB
    random_rank = jax.random.randint(jax.random.fold_in(own_key, 1), (SB, TB), 0, 2 ** 19, dtype=jnp.int32)
    offsets = jnp.arange(TB, dtype=jnp.int32)
    forced = jnp.where(offsets % SB == 0, 2 ** 30, 0).astype(jnp.int32)
    ranked = random_rank * TB + offsets[None, :] + forced[None, :]
    _, chosen = lax.top_k(ranked, K)
    columns = (jnp.arange(SB, dtype=jnp.int32)[:, None] + chosen.astype(jnp.int32)) % TB
    levels = jax.random.randint(jax.random.fold_in(own_key, 2), (SB // BR_DEV,), 1, 5, dtype=jnp.int32)
    levels = jnp.repeat(levels, BR_DEV)
    spread = jax.random.randint(jax.random.fold_in(own_key, 3), (SB,), (K - reaching) // 2, K - reaching + 1, dtype=jnp.int32)
    counts = jnp.minimum(K, reaching + spread * levels // 4)
    counts = counts.at[0].set(K).at[SB - 1].set(reaching)
    return (columns.astype(jnp.int32), counts.astype(jnp.int32))


def draw_source_features(key, part):
    own_key = jax.random.fold_in(key, 3)
    values = 0.5 * jnp.clip(jax.random.normal(own_key, (NS, FEAT), jnp.float32), -8.0, 8.0)
    return values.astype(jnp.bfloat16)


def draw_target_features(key, part):
    return target_values(key).astype(jnp.bfloat16)


def draw_block_columns(key, part):
    return support(key)[0]


def draw_block_counts(key, part):
    return support(key)[1]


def level_of(key, dims, split, low, high):
    def one(position, shards_of):
        steps = jax.random.uniform(jax.random.fold_in(jax.random.fold_in(key, 6), position), (shards_of,), jnp.float32, low / len(split), high / len(split))
        return jnp.repeat(jnp.exp(steps), dims[position] // shards_of).reshape((-1,) + (1,) * (len(dims) - position - 1))

    level = one(*split[0])
    for cut in split[1:]:
        level = level * one(*cut)
    return level


def setup_inputs(seed: int = 0, part: int = 0) -> dict:
    keys = jax.random.split(jax.random.key(seed), 7)
    part_keys = jax.random.split(jax.random.fold_in(keys[6], part), 7)
    source_features = draw_source_features(jax.random.fold_in(jax.random.fold_in(keys[6], part), 71), part)
    target_features = draw_target_features(jax.random.fold_in(jax.random.fold_in(keys[6], part), 71), part)
    source_weights = jnp.clip(jax.random.uniform(part_keys[2], (NS,), jnp.float32, -1.0, 1.0) * level_of(part_keys[2], (NS,), ((0, 16),), -0.4, 0.0), -1.0, 1.0)
    target_weights = jnp.clip(jax.random.uniform(part_keys[3], (NT,), jnp.float32, -1.0, 1.0), -1.0, 1.0)
    block_columns = draw_block_columns(jax.random.fold_in(jax.random.fold_in(keys[6], part), 71), part)
    block_counts = draw_block_counts(jax.random.fold_in(jax.random.fold_in(keys[6], part), 71), part)
    return dict(source_features=source_features, target_features=target_features, source_weights=source_weights, target_weights=target_weights, block_columns=block_columns, block_counts=block_counts)


EPSILON = 1.0
FLOOR = -1e30


def block_scores(source_block, target_blocks, columns):
    picked = target_blocks[columns].astype(jnp.float32)
    return jnp.einsum("rf,kcf->rkc", source_block.astype(jnp.float32), picked) / EPSILON


def reference(source_features, target_features, source_weights, target_weights, block_columns, block_counts):
    source_blocks = source_features.reshape(SB, BLOCK, FEAT)
    target_blocks = target_features.reshape(TB, BLOCK, FEAT)
    usable = jnp.arange(K, dtype=jnp.int32)[None, :] < block_counts[:, None]
    weights_src = source_weights.reshape(SB, BLOCK)
    weights_tgt = target_weights.reshape(TB, BLOCK)
    source_pot = jnp.zeros((SB, BLOCK), jnp.float32)
    target_pot = jnp.zeros((TB, BLOCK), jnp.float32)
    for sweep in range(ITERS):
        def column_step(carry, which):
            running_max, running_sum = carry
            columns = block_columns[which]
            scores = block_scores(source_blocks[which], target_blocks, columns) + source_pot[which][:, None, None]
            block_max = jnp.max(scores, axis=0)
            block_sum = jnp.sum(jnp.exp(scores - block_max[None]), axis=0)
            keep = usable[which][:, None]
            block_max = jnp.where(keep, block_max, FLOOR)
            block_sum = jnp.where(keep, block_sum, 0.0)
            old_max = running_max[columns]
            old_sum = running_sum[columns]
            new_max = jnp.maximum(old_max, block_max)
            new_sum = old_sum * jnp.exp(old_max - new_max) + block_sum * jnp.exp(block_max - new_max)
            return (running_max.at[columns].set(new_max), running_sum.at[columns].set(new_sum)), None

        start = (jnp.full((TB, BLOCK), FLOOR, jnp.float32), jnp.zeros((TB, BLOCK), jnp.float32))
        (running_max, running_sum), _ = lax.scan(column_step, start, jnp.arange(SB, dtype=jnp.int32))
        target_pot = weights_tgt - (running_max + jnp.log(running_sum))

        def row_step(which):
            columns = block_columns[which]
            scores = block_scores(source_blocks[which], target_blocks, columns) + target_pot[columns][None]
            scores = jnp.where(usable[which][None, :, None], scores, FLOOR)
            top = jnp.max(scores, axis=(1, 2))
            summed = jnp.sum(jnp.exp(scores - top[:, None, None]), axis=(1, 2))
            return weights_src[which] - (top + jnp.log(summed))

        source_pot = lax.map(row_step, jnp.arange(SB, dtype=jnp.int32))
    return source_pot.reshape(NS), target_pot.reshape(NT)
```

```python
import functools

import jax
import jax.numpy as jnp
from jax import lax
from jax.experimental import pallas as pl
from jax.experimental.pallas import tpu as pltpu
from jax.sharding import PartitionSpec as P

BLOCK = 256
ITERS = 3
FLOOR = -1e30
GROUP = 2
ROWS = 32
VMEM_BYTES = 52 * 1024 * 1024


def scores_of(source_ref, gathered, which, slot, slots):
    source = source_ref[pl.ds(pl.multiple_of(which * BLOCK, BLOCK), BLOCK), :]
    return jnp.dot(source, gathered[which * slots + slot], preferred_element_type=jnp.float32)


def fetch(columns_ref, targets_ref, gathered, sems, which, slot, slots):
    column = columns_ref[which, slot]
    return pltpu.make_async_copy(
        targets_ref.at[:, pl.ds(pl.multiple_of(column * BLOCK, BLOCK), BLOCK)],
        gathered.at[which * slots + slot],
        sems.at[which * slots + slot],
    )


def rounded(count):
    return (count + GROUP - 1) // GROUP


def start_all(columns_ref, counts_ref, targets_ref, gathered, sems):
    own, slots = columns_ref.shape

    def one_source(which, _):
        def one(slot, _):
            fetch(columns_ref, targets_ref, gathered, sems, which, slot, slots).start()
            return 0

        return lax.fori_loop(0, rounded(counts_ref[which]) * GROUP, one, 0)

    lax.fori_loop(0, own, one_source, 0)


def row_of(columns_ref, counts_ref, which, slot, target_count):
    return jnp.where(slot < counts_ref[which], columns_ref[which, slot], target_count)


def clear(ref, target_count, value):
    own = ref.shape[0]

    def one(i, _):
        rows = pl.ds(pl.multiple_of(i * ROWS, ROWS), ROWS)
        for p in range(own):
            ref[p, rows, :] = jnp.full((ROWS, BLOCK), value, jnp.float32)
        return 0

    lax.fori_loop(0, target_count // ROWS, one, 0)


def first_columns(
    columns_ref, counts_ref, source_ref, targets_ref, out_ref, gathered, tops, sums, sems
):
    own, slots = columns_ref.shape
    target_count = out_ref.shape[0]
    start_all(columns_ref, counts_ref, targets_ref, gathered, sems)
    clear(tops, target_count, FLOOR)
    clear(sums, target_count, 0.0)

    def one_source(which, _):
        def group(i, _):
            for k in range(GROUP):
                slot = i * GROUP + k
                fetch(columns_ref, targets_ref, gathered, sems, which, slot, slots).wait()
            for k in range(GROUP):
                slot = i * GROUP + k
                scores = scores_of(source_ref, gathered, which, slot, slots)
                top = jnp.max(scores, axis=0, keepdims=True)
                total = jnp.sum(jnp.exp(scores - top), axis=0, keepdims=True)
                row = row_of(columns_ref, counts_ref, which, slot, target_count)
                tops[which, pl.ds(row, 1), :] = top
                sums[which, pl.ds(row, 1), :] = total
            return 0

        return lax.fori_loop(0, rounded(counts_ref[which]), group, 0)

    lax.fori_loop(0, own, one_source, 0)

    def combine(i, _):
        rows = pl.ds(pl.multiple_of(i * ROWS, ROWS), ROWS)
        top = tops[0, rows, :]
        for p in range(1, own):
            top = jnp.maximum(top, tops[p, rows, :])
        total = jnp.zeros_like(top)
        for p in range(own):
            total = total + sums[p, rows, :] * jnp.exp(tops[p, rows, :] - top)
        used = total > 0.0
        out_ref[rows, :] = jnp.where(used, top + jnp.log(jnp.where(used, total, 1.0)), FLOOR)
        return 0

    lax.fori_loop(0, target_count // ROWS, combine, 0)


def halves(x):
    return x[:, : BLOCK // 2], x[:, BLOCK // 2 :]


def rows_kernel(
    first,
    columns_out,
    columns_ref,
    counts_ref,
    source_ref,
    weights_ref,
    old_ref,
    pot_ref,
    targets_ref,
    new_ref,
    *rest,
):
    if columns_out:
        out_ref, gathered, held, partial, sems, dense = rest
    else:
        gathered, held, partial, sems = rest
    own, slots = columns_ref.shape
    target_count = pot_ref.shape[0]
    start_all(columns_ref, counts_ref, targets_ref, gathered, sems)
    if columns_out:
        clear(dense, target_count, 0.0)

    def one_source(which, _):
        own_rows = pl.ds(pl.multiple_of(which * BLOCK, BLOCK), BLOCK)
        groups = rounded(counts_ref[which])

        def wait(i):
            for k in range(GROUP):
                slot = i * GROUP + k
                fetch(columns_ref, targets_ref, gathered, sems, which, slot, slots).wait()

        def shifted(slot):
            scores = scores_of(source_ref, gathered, which, slot, slots)
            column = columns_ref[which, slot]
            pot = pot_ref[pl.ds(column, 1), :] + jnp.where(slot < counts_ref[which], 0.0, FLOOR)
            return scores + pot

        if first:
            partial[...] = jnp.full(partial.shape, FLOOR, jnp.float32)

            def top_group(i, _):
                wait(i)
                best = partial[...]
                for k in range(GROUP):
                    low, high = halves(shifted(i * GROUP + k))
                    best = jnp.maximum(best, jnp.maximum(low, high))
                partial[...] = best
                return 0

            lax.fori_loop(0, groups, top_group, 0)
            offset = -jnp.max(partial[...], axis=1, keepdims=True)
        else:
            offset = old_ref[own_rows, :]

        partial[...] = jnp.zeros(partial.shape, jnp.float32)

        def sum_group(i, _):
            if not first:
                wait(i)
            total = partial[...]
            for k in range(GROUP):
                slot = i * GROUP + k
                terms = jnp.exp(shifted(slot) + offset)
                if columns_out:
                    held[slot] = terms
                low, high = halves(terms)
                total = total + (low + high)
            partial[...] = total
            return 0

        lax.fori_loop(0, groups, sum_group, 0)
        total = jnp.sum(partial[...], axis=1, keepdims=True)
        weights = weights_ref[own_rows, :]
        new_ref[own_rows, :] = weights + offset - jnp.log(total)
        if columns_out:
            factor = jnp.exp(weights) / total

            def column_group(i, _):
                for k in range(GROUP):
                    slot = i * GROUP + k
                    row = row_of(columns_ref, counts_ref, which, slot, target_count)
                    dense[which, pl.ds(row, 1), :] = jnp.sum(
                        held[slot] * factor, axis=0, keepdims=True
                    )
                return 0

            lax.fori_loop(0, groups, column_group, 0)
        return 0

    lax.fori_loop(0, own, one_source, 0)

    if columns_out:

        def combine(i, _):
            rows = pl.ds(pl.multiple_of(i * ROWS, ROWS), ROWS)
            total = dense[0, rows, :]
            for p in range(1, own):
                total = total + dense[p, rows, :]
            out_ref[rows, :] = total
            return 0

        lax.fori_loop(0, target_count // ROWS, combine, 0)


def stages_of(devices):
    radices = []
    rest = devices
    if rest % 2 == 0:
        radices.append(2)
        rest //= 2
    while rest > 1:
        if rest % 4 == 0 and (rest & (rest - 1)) == 0 and rest.bit_length() % 2 == 1:
            radix = 4
        elif rest % 2 == 0:
            radix = 2
        else:
            radix = rest
        radices.append(radix)
        rest //= radix
    stages = []
    stride = 1
    for radix in radices:
        stages.append((radix, stride))
        stride *= radix
    return stages


def reduce_kernel(
    first,
    stages,
    term_ref,
    weights_ref,
    old_ref,
    out_ref,
    total,
    landed,
    weights_own,
    old_own,
    send_sems,
    recv_sems,
    local_sems,
):
    me = lax.axis_index("row")
    barrier = pltpu.get_barrier_semaphore()
    greeted = 0
    for radix, stride in stages:
        digit = lax.rem(me // stride, radix)
        for k in range(1, radix):
            peer = me + (lax.rem(digit + k, radix) - digit) * stride
            pl.semaphore_signal(
                barrier, inc=1, device_id={"row": peer}, device_id_type=pl.DeviceIdType.MESH
            )
            greeted += 1
    length = term_ref.shape[0]
    base = 0
    bases = []
    for radix, stride in stages:
        bases.append(base)
        length //= radix
        base = base + lax.rem(me // stride, radix) * length
    own = pl.ds(pl.multiple_of(base, 8), length)
    local = [pltpu.make_async_copy(weights_ref.at[own], weights_own, local_sems.at[0])]
    if not first:
        local.append(pltpu.make_async_copy(old_ref.at[own], old_own, local_sems.at[1]))
    for copy in local:
        copy.start()
    pl.semaphore_wait(barrier, greeted)

    sent = []
    index = 0
    offset = 0
    piece = term_ref.shape[0]
    current = term_ref
    for number, (radix, stride) in enumerate(stages):
        digit = lax.rem(me // stride, radix)
        piece //= radix
        copies = []
        for k in range(1, radix):
            other = lax.rem(digit + k, radix)
            peer = me + (other - digit) * stride
            start = pl.multiple_of(bases[number] + other * piece, 8)
            copy = pltpu.make_async_remote_copy(
                src_ref=current.at[pl.ds(start, piece)],
                dst_ref=landed.at[pl.ds(offset + (k - 1) * piece, piece)],
                send_sem=send_sems.at[index],
                recv_sem=recv_sems.at[index],
                device_id={"row": peer},
                device_id_type=pl.DeviceIdType.MESH,
            )
            copy.start()
            copies.append(copy)
            index += 1
        for copy in copies:
            copy.wait_recv()
        sent += copies
        mine = bases[number] + digit * piece

        def fold(i, _, mine=mine, offset=offset, radix=radix, piece=piece, current=current):
            rows = pl.ds(pl.multiple_of(mine + i * ROWS, 8), ROWS)
            parts = [current[rows, :]]
            for k in range(1, radix):
                start = pl.multiple_of(offset + (k - 1) * piece + i * ROWS, 8)
                parts.append(landed[pl.ds(start, ROWS), :])
            if first:
                top = functools.reduce(jnp.maximum, parts)
                value = top + jnp.log(sum(jnp.exp(part - top) for part in parts))
            else:
                value = sum(parts[1:], parts[0])
            total[rows, :] = value
            return 0

        lax.fori_loop(0, piece // ROWS, fold, 0)
        offset += (radix - 1) * piece
        current = total

    for copy in local:
        copy.wait()

    def finish(i, _):
        rows = pl.ds(pl.multiple_of(base + i * ROWS, 8), ROWS)
        near = pl.ds(pl.multiple_of(i * ROWS, 8), ROWS)
        if first:
            out_ref[rows, :] = weights_own[near, :] - total[rows, :]
        else:
            out_ref[rows, :] = weights_own[near, :] + old_own[near, :] - jnp.log(total[rows, :])
        return 0

    lax.fori_loop(0, piece // ROWS, finish, 0)

    start = base
    for number in reversed(range(len(stages))):
        radix, stride = stages[number]
        digit = lax.rem(me // stride, radix)
        rows = pl.ds(pl.multiple_of(start, 8), piece)
        copies = []
        for k in range(1, radix):
            peer = me + (lax.rem(digit + k, radix) - digit) * stride
            copy = pltpu.make_async_remote_copy(
                src_ref=out_ref.at[rows],
                dst_ref=out_ref.at[rows],
                send_sem=send_sems.at[index],
                recv_sem=recv_sems.at[index],
                device_id={"row": peer},
                device_id_type=pl.DeviceIdType.MESH,
            )
            copy.start()
            copies.append(copy)
            index += 1
        for copy in copies:
            copy.wait_recv()
        sent += copies
        start = bases[number]
        piece *= radix
    for copy in sent:
        copy.wait_send()


def local(
    source_features, target_features, source_weights, target_weights, block_columns, block_counts
):
    own, slots = block_columns.shape
    target_count = target_features.shape[0] // BLOCK
    width = target_features.shape[1]
    cells = source_features.shape[0]
    devices = lax.axis_size("row")
    stages = stages_of(devices)
    share = target_count // devices
    targets = target_features.T
    weights_tgt = target_weights.reshape(target_count, BLOCK)
    weights_src = source_weights.reshape(cells, 1)

    in_smem = pl.BlockSpec(memory_space=pltpu.SMEM)
    in_vmem = pl.BlockSpec(memory_space=pltpu.VMEM)
    anywhere = pl.BlockSpec(memory_space=pl.ANY)
    params = pltpu.CompilerParams(vmem_limit_bytes=VMEM_BYTES)
    gathered = pltpu.VMEM((own * slots, width, BLOCK), source_features.dtype)
    fetches = pltpu.SemaphoreType.DMA((own * slots,))
    dense = pltpu.VMEM((own, target_count + 8, BLOCK), jnp.float32)
    whole = jax.ShapeDtypeStruct((target_count, BLOCK), jnp.float32)
    per_source = jax.ShapeDtypeStruct((cells, 1), jnp.float32)

    first_term = pl.pallas_call(
        first_columns,
        out_shape=whole,
        in_specs=[in_smem, in_smem, in_vmem, anywhere],
        out_specs=in_vmem,
        scratch_shapes=[gathered, dense, dense, fetches],
        compiler_params=params,
        name="first_columns",
    )

    def rows(first, columns_out):
        scratch = [
            gathered,
            pltpu.VMEM((slots, BLOCK, BLOCK), jnp.float32),
            pltpu.VMEM((BLOCK, BLOCK // 2), jnp.float32),
            fetches,
        ]
        return pl.pallas_call(
            functools.partial(rows_kernel, first, columns_out),
            out_shape=(per_source, whole) if columns_out else per_source,
            in_specs=[in_smem, in_smem, in_vmem, in_vmem, in_vmem, in_vmem, anywhere],
            out_specs=(in_vmem, in_vmem) if columns_out else in_vmem,
            scratch_shapes=scratch + ([dense] if columns_out else []),
            compiler_params=params,
            name="rows",
        )

    messages = 2 * sum(radix - 1 for radix, _ in stages)
    landing = 0
    piece = target_count
    for radix, _ in stages:
        piece //= radix
        landing += (radix - 1) * piece

    def reduce_call(first):
        return pl.pallas_call(
            functools.partial(reduce_kernel, first, stages),
            out_shape=whole,
            in_specs=[in_vmem, anywhere, anywhere],
            out_specs=in_vmem,
            scratch_shapes=[
                pltpu.VMEM((target_count, BLOCK), jnp.float32),
                pltpu.VMEM((landing, BLOCK), jnp.float32),
                pltpu.VMEM((share, BLOCK), jnp.float32),
                pltpu.VMEM((share, BLOCK), jnp.float32),
                pltpu.SemaphoreType.DMA((messages,)),
                pltpu.SemaphoreType.DMA((messages,)),
                pltpu.SemaphoreType.DMA((2,)),
            ],
            compiler_params=pltpu.CompilerParams(
                vmem_limit_bytes=VMEM_BYTES,
                collective_id=0 if first else 1,
                has_side_effects=True,
            ),
            name="reduce",
        )

    term = first_term(block_columns, block_counts, source_features, targets)
    target_pot = reduce_call(True)(term, weights_tgt, weights_tgt)
    source_pot = weights_src
    for sweep in range(ITERS):
        last = sweep == ITERS - 1
        result = rows(sweep == 0, not last)(
            block_columns, block_counts, source_features, weights_src, source_pot, target_pot, targets
        )
        if last:
            source_pot = result
        else:
            source_pot, term = result
            target_pot = reduce_call(False)(term, weights_tgt, target_pot)
    position = lax.axis_index("row")
    own_pot = lax.dynamic_slice_in_dim(target_pot, position * share, share, 0)
    return (source_pot.reshape(-1), own_pot.reshape(-1))


def solution(mesh):
    return jax.shard_map(
        local,
        mesh=mesh,
        in_specs=(
            P(("groups", "row"), None),
            P("groups", None),
            P(("groups", "row")),
            P("groups"),
            P(("groups", "row"), None),
            P(("groups", "row")),
        ),
        out_specs=(P(("groups", "row")), P(("groups", "row"))),
        check_vma=False,
    )
```

```python
import functools

import jax
import jax.numpy as jnp
from jax import lax
from jax.experimental import pallas as pl
from jax.experimental.pallas import tpu as pltpu
from jax.sharding import PartitionSpec as P

BLOCK = 256
ITERS = 3
FLOOR = -1e30
GROUP = 16
ROWS = 32
AHEAD = 2
CHUNKS = 2
EXTRA = 16
HALVES = (pl.ds(0, BLOCK // 2), pl.ds(BLOCK // 2, BLOCK // 2))
VMEM_BYTES = 50 * 1024 * 1024


def scores_of(source_ref, gathered, which, slot, slots, lanes):
    width = gathered.shape[1]
    source = source_ref[pl.ds(pl.multiple_of(which * BLOCK, BLOCK), BLOCK), pl.ds(0, width)]
    targets = gathered[which * slots + slot, :, lanes]
    return jnp.dot(source, targets, preferred_element_type=jnp.float32)


def pieces(x):
    high = x.astype(jnp.bfloat16).astype(jnp.float32)
    rest = x - high
    middle = rest.astype(jnp.bfloat16).astype(jnp.float32)
    return high, middle, rest - middle


def with_pieces(x, index, at, base):
    for k, piece in enumerate(pieces(x)):
        base = jnp.where(index == at + k, piece, base)
    return base


def fetch(columns_ref, targets_ref, gathered, sems, index):
    slots = columns_ref.shape[1]
    column = columns_ref[index // slots, lax.rem(index, slots)]
    return pltpu.make_async_copy(
        targets_ref.at[:, pl.ds(pl.multiple_of(column * BLOCK, BLOCK), BLOCK)],
        gathered.at[index],
        sems.at[index],
    )


def row_of(columns_ref, counts_ref, which, slot, target_count):
    return jnp.where(slot < counts_ref[which], columns_ref[which, slot], target_count)


def clear(ref, target_count, value):
    own = ref.shape[0]

    def one(i, _):
        rows = pl.ds(pl.multiple_of(i * ROWS, ROWS), ROWS)
        for p in range(own):
            ref[p, rows, :] = jnp.full((ROWS, BLOCK), value, jnp.float32)
        return 0

    lax.fori_loop(0, target_count // ROWS, one, 0)


def first_columns(
    columns_ref, counts_ref, source_ref, targets_ref, out_ref, gathered, tops, sums, sems
):
    own, slots = columns_ref.shape
    target_count = out_ref.shape[0]
    groups = own * slots // GROUP

    def start(group):
        for k in range(GROUP):
            fetch(columns_ref, targets_ref, gathered, sems, group * GROUP + k).start()

    for group in range(min(AHEAD, groups)):
        start(group)
    clear(tops, target_count, FLOOR)
    clear(sums, target_count, 0.0)

    def work(group):
        for k in range(GROUP):
            fetch(columns_ref, targets_ref, gathered, sems, group * GROUP + k).wait()
        which = group * GROUP // slots
        for k in range(GROUP):
            slot = lax.rem(group * GROUP, slots) + k
            row = row_of(columns_ref, counts_ref, which, slot, target_count)
            top_parts = []
            sum_parts = []
            for lanes in HALVES:
                scores = scores_of(source_ref, gathered, which, slot, slots, lanes)
                top = jnp.max(scores, axis=0, keepdims=True)
                top_parts.append(top)
                sum_parts.append(jnp.sum(jnp.exp(scores - top), axis=0, keepdims=True))
            tops[which, pl.ds(row, 1), :] = jnp.concatenate(top_parts, axis=1)
            sums[which, pl.ds(row, 1), :] = jnp.concatenate(sum_parts, axis=1)

    def ahead(group, _):
        start(group + AHEAD)
        work(group)
        return 0

    def rest(group, _):
        work(group)
        return 0

    full = max(groups - AHEAD, 0)
    lax.fori_loop(0, full, ahead, 0)
    lax.fori_loop(full, groups, rest, 0)

    def combine(i, _):
        rows = pl.ds(pl.multiple_of(i * ROWS, ROWS), ROWS)
        top = tops[0, rows, :]
        for p in range(1, own):
            top = jnp.maximum(top, tops[p, rows, :])
        total = jnp.zeros_like(top)
        for p in range(own):
            total = total + sums[p, rows, :] * jnp.exp(tops[p, rows, :] - top)
        used = total > 0.0
        out_ref[rows, :] = jnp.where(used, top + jnp.log(jnp.where(used, total, 1.0)), FLOOR)
        return 0

    lax.fori_loop(0, target_count // ROWS, combine, 0)


def halves(x):
    return x[:, : BLOCK // 2], x[:, BLOCK // 2 :]


def rows_kernel(
    first,
    columns_out,
    columns_ref,
    counts_ref,
    source_ref,
    weights_ref,
    old_ref,
    pot_ref,
    gathered,
    new_ref,
    *rest,
):
    if columns_out:
        out_ref, held, partial, source, dense = rest
    else:
        own_ref, partial, source = rest
    own, slots = columns_ref.shape
    target_count = pot_ref.shape[0]
    if columns_out:
        clear(dense, target_count, 0.0)
    else:
        share = own_ref.shape[0]
        mine = pl.multiple_of(lax.axis_index("row") * share, 8)
        own_ref[...] = pot_ref[pl.ds(mine, share), :]
    width = gathered.shape[1]
    extra_row = lax.broadcasted_iota(jnp.int32, (EXTRA, BLOCK), 0)
    ones = jnp.where(extra_row < 3, 1.0, 0.0)
    lane = lax.broadcasted_iota(jnp.int32, (BLOCK, width + EXTRA), 1)

    def one_source(which, _):
        own_rows = pl.ds(pl.multiple_of(which * BLOCK, BLOCK), BLOCK)
        groups = slots // GROUP

        def set_source(offset):
            base = source_ref[own_rows, :].astype(jnp.float32)
            source[...] = with_pieces(offset, lane, width, base).astype(source.dtype)

        def shifted(slot):
            column = columns_ref[which, slot]
            pot = pot_ref[pl.ds(column, 1), :] + jnp.where(slot < counts_ref[which], 0.0, FLOOR)
            extra = with_pieces(pot, extra_row, 3, ones).astype(source.dtype)
            targets = jnp.concatenate([gathered[which * slots + slot], extra], axis=0)
            return jnp.dot(source[...], targets, preferred_element_type=jnp.float32)

        if first:
            set_source(jnp.zeros((BLOCK, 1), jnp.float32))
            partial[...] = jnp.full(partial.shape, FLOOR, jnp.float32)

            def top_group(i, _):
                best = partial[...]
                for k in range(GROUP):
                    low, high = halves(shifted(i * GROUP + k))
                    best = jnp.maximum(best, jnp.maximum(low, high))
                partial[...] = best
                return 0

            lax.fori_loop(0, groups, top_group, 0)
            offset = -jnp.max(partial[...], axis=1, keepdims=True)
        else:
            offset = old_ref[own_rows, :]

        set_source(offset)
        partial[...] = jnp.zeros(partial.shape, jnp.float32)

        def sum_group(i, _):
            total = partial[...]
            for k in range(GROUP):
                slot = i * GROUP + k
                terms = jnp.exp(shifted(slot))
                if columns_out:
                    held[slot] = terms
                low, high = halves(terms)
                total = total + (low + high)
            partial[...] = total
            return 0

        lax.fori_loop(0, groups, sum_group, 0)
        total = jnp.sum(partial[...], axis=1, keepdims=True)
        weights = weights_ref[own_rows, :]
        new_ref[own_rows, :] = weights + offset - jnp.log(total)
        if columns_out:
            partial[...] = jnp.broadcast_to(jnp.exp(weights) / total, partial.shape)

            def column_group(i, _):
                factor = partial[...]
                for k in range(GROUP):
                    slot = i * GROUP + k
                    row = row_of(columns_ref, counts_ref, which, slot, target_count)
                    parts = [
                        jnp.sum(held[slot, :, lanes] * factor, axis=0, keepdims=True)
                        for lanes in HALVES
                    ]
                    dense[which, pl.ds(row, 1), :] = jnp.concatenate(parts, axis=1)
                return 0

            lax.fori_loop(0, groups, column_group, 0)
        return 0

    lax.fori_loop(0, own, one_source, 0)

    if columns_out:

        def combine(i, _):
            rows = pl.ds(pl.multiple_of(i * ROWS, ROWS), ROWS)
            total = dense[0, rows, :]
            for p in range(1, own):
                total = total + dense[p, rows, :]
            out_ref[rows, :] = total
            return 0

        lax.fori_loop(0, target_count // ROWS, combine, 0)


def stages_of(devices):
    radices = []
    rest = devices
    if rest % 2 == 0:
        radices.append(2)
        rest //= 2
    while rest > 1:
        if rest % 4 == 0 and (rest & (rest - 1)) == 0 and rest.bit_length() % 2 == 1:
            radix = 4
        elif rest % 2 == 0:
            radix = 2
        else:
            radix = rest
        radices.append(radix)
        rest //= radix
    stages = []
    stride = 1
    for radix in radices:
        stages.append((radix, stride))
        stride *= radix
    return stages


def reduce_kernel(
    first,
    stages,
    term_ref,
    weights_ref,
    old_ref,
    out_ref,
    total,
    landed,
    weights_own,
    old_own,
    send_sems,
    recv_sems,
    local_sems,
):
    me = lax.axis_index("row")
    barrier = pltpu.get_barrier_semaphore()
    greeted = 0
    for radix, stride in stages:
        digit = lax.rem(me // stride, radix)
        for k in range(1, radix):
            peer = me + (lax.rem(digit + k, radix) - digit) * stride
            pl.semaphore_signal(
                barrier, inc=1, device_id={"row": peer}, device_id_type=pl.DeviceIdType.MESH
            )
            greeted += 1
    chunk = term_ref.shape[0] // CHUNKS
    share = chunk
    for radix, _ in stages:
        share //= radix
    orders = []
    bases = []
    for c in range(CHUNKS):
        rest = stages[1:]
        turn = c % len(rest) if rest else 0
        orders.append(stages[:1] + rest[turn:] + rest[:turn])
        base = c * chunk
        piece = chunk
        levels = [base]
        for radix, stride in orders[c]:
            piece //= radix
            base = base + lax.rem(me // stride, radix) * piece
            levels.append(base)
        bases.append(levels)
    local = []
    for c in range(CHUNKS):
        rows = pl.ds(pl.multiple_of(bases[c][-1], 8), share)
        near = pl.ds(c * share, share)
        sources = [(weights_ref, weights_own)] if first else [
            (weights_ref, weights_own), (old_ref, old_own)
        ]
        for source, target in sources:
            local.append(
                pltpu.make_async_copy(source.at[rows], target.at[near], local_sems.at[len(local)])
            )
    for copy in local:
        copy.start()
    pl.semaphore_wait(barrier, greeted)

    sent = []

    def send(source, start, target, target_start, size, peer):
        index = len(sent)
        copy = pltpu.make_async_remote_copy(
            src_ref=source.at[pl.ds(pl.multiple_of(start, 8), size)],
            dst_ref=target.at[pl.ds(pl.multiple_of(target_start, 8), size)],
            send_sem=send_sems.at[index],
            recv_sem=recv_sems.at[index],
            device_id={"row": peer},
            device_id_type=pl.DeviceIdType.MESH,
        )
        copy.start()
        sent.append(copy)
        return copy

    flying = [[] for _ in range(CHUNKS)]
    places = [0] * CHUNKS
    sizes = [chunk] * CHUNKS
    offset = 0

    def fold(c, number):
        radix, _ = orders[c][number]
        size = sizes[c]
        step = min(ROWS, size)
        mine = bases[c][number + 1]
        place = places[c]
        current = term_ref if number == 0 else total
        last = number == len(stages) - 1

        def one(i, _):
            rows = pl.ds(pl.multiple_of(mine + i * step, 8), step)
            parts = [current[rows, :]]
            for k in range(1, radix):
                start = pl.multiple_of(place + (k - 1) * size + i * step, 8)
                parts.append(landed[pl.ds(start, step), :])
            if first:
                top = functools.reduce(jnp.maximum, parts)
                value = top + jnp.log(sum(jnp.exp(part - top) for part in parts))
            else:
                value = sum(parts[1:], parts[0])
            if last:
                near = pl.ds(pl.multiple_of(c * share + i * step, 8), step)
                if first:
                    out_ref[rows, :] = weights_own[near, :] - value
                else:
                    out_ref[rows, :] = weights_own[near, :] + old_own[near, :] - jnp.log(value)
            else:
                total[rows, :] = value
            return 0

        lax.fori_loop(0, size // step, one, 0)

    for number in range(len(stages) + 1):
        if number == len(stages):
            for copy in local:
                copy.wait()
        for c in range(CHUNKS):
            for copy in flying[c]:
                copy.wait_recv()
            if number > 0:
                fold(c, number - 1)
            if number == len(stages):
                continue
            radix, stride = orders[c][number]
            digit = lax.rem(me // stride, radix)
            sizes[c] //= radix
            places[c] = offset
            flying[c] = []
            for k in range(1, radix):
                other = lax.rem(digit + k, radix)
                flying[c].append(
                    send(
                        term_ref if number == 0 else total,
                        bases[c][number] + other * sizes[c],
                        landed,
                        offset,
                        sizes[c],
                        me + (other - digit) * stride,
                    )
                )
                offset += sizes[c]

    flying = [[] for _ in range(CHUNKS)]
    for number in reversed(range(len(stages))):
        for c in range(CHUNKS):
            for copy in flying[c]:
                copy.wait_recv()
            radix, stride = orders[c][number]
            digit = lax.rem(me // stride, radix)
            start = bases[c][number + 1]
            flying[c] = []
            for k in range(1, radix):
                other = lax.rem(digit + k, radix)
                flying[c].append(
                    send(out_ref, start, out_ref, start, sizes[c], me + (other - digit) * stride)
                )
            sizes[c] *= radix
    for c in range(CHUNKS):
        for copy in flying[c]:
            copy.wait_recv()
    for copy in sent:
        copy.wait_send()


def local(
    source_features, target_features, source_weights, target_weights, block_columns, block_counts
):
    own, slots = block_columns.shape
    target_count = target_features.shape[0] // BLOCK
    width = target_features.shape[1]
    cells = source_features.shape[0]
    carriers = jnp.broadcast_to(
        jnp.where((jnp.arange(EXTRA) >= 3) & (jnp.arange(EXTRA) < 6), 1.0, 0.0), (cells, EXTRA)
    )
    sources = jnp.concatenate([source_features, carriers.astype(source_features.dtype)], axis=1)
    devices = lax.axis_size("row")
    stages = stages_of(devices)
    share = target_count // devices
    targets = target_features.T
    weights_tgt = target_weights.reshape(target_count, BLOCK)
    weights_src = source_weights.reshape(cells, 1)

    in_smem = pl.BlockSpec(memory_space=pltpu.SMEM)
    in_vmem = pl.BlockSpec(memory_space=pltpu.VMEM)
    anywhere = pl.BlockSpec(memory_space=pl.ANY)
    in_hbm = pl.BlockSpec(memory_space=pltpu.HBM)
    params = pltpu.CompilerParams(vmem_limit_bytes=VMEM_BYTES)
    gathered = jax.ShapeDtypeStruct((own * slots, width, BLOCK), source_features.dtype)
    fetches = pltpu.SemaphoreType.DMA((own * slots,))
    dense = pltpu.VMEM((own, target_count + 8, BLOCK), jnp.float32)
    whole = jax.ShapeDtypeStruct((target_count, BLOCK), jnp.float32)
    part = jax.ShapeDtypeStruct((share, BLOCK), jnp.float32)
    per_source = jax.ShapeDtypeStruct((cells, 1), jnp.float32)

    first_term = pl.pallas_call(
        first_columns,
        out_shape=(whole, gathered),
        in_specs=[in_smem, in_smem, in_vmem, in_hbm],
        out_specs=(in_vmem, in_vmem),
        scratch_shapes=[dense, dense, fetches],
        compiler_params=params,
        name="first_columns",
    )

    def rows(first, columns_out):
        partial = pltpu.VMEM((BLOCK, BLOCK // 2), jnp.float32)
        source = pltpu.VMEM((BLOCK, width + EXTRA), source_features.dtype)
        held = pltpu.VMEM((slots, BLOCK, BLOCK), jnp.float32)
        return pl.pallas_call(
            functools.partial(rows_kernel, first, columns_out),
            out_shape=(per_source, whole if columns_out else part),
            in_specs=[in_smem, in_smem, in_vmem, in_vmem, in_vmem, in_vmem, in_vmem],
            out_specs=(in_vmem, in_vmem),
            scratch_shapes=[held, partial, source, dense] if columns_out else [partial, source],
            compiler_params=params,
            name="rows",
        )

    messages = 2 * CHUNKS * sum(radix - 1 for radix, _ in stages)

    def reduce_call(first):
        return pl.pallas_call(
            functools.partial(reduce_kernel, first, stages),
            out_shape=whole,
            in_specs=[in_vmem, anywhere, anywhere],
            out_specs=in_vmem,
            scratch_shapes=[
                pltpu.VMEM((target_count, BLOCK), jnp.float32),
                pltpu.VMEM((target_count, BLOCK), jnp.float32),
                pltpu.VMEM((share, BLOCK), jnp.float32),
                pltpu.VMEM((share, BLOCK), jnp.float32),
                pltpu.SemaphoreType.DMA((messages,)),
                pltpu.SemaphoreType.DMA((messages,)),
                pltpu.SemaphoreType.DMA((2 * CHUNKS,)),
            ],
            compiler_params=pltpu.CompilerParams(
                vmem_limit_bytes=VMEM_BYTES,
                collective_id=0 if first else 1,
                has_side_effects=True,
            ),
            name="reduce",
        )

    term, picked = first_term(block_columns, block_counts, sources, targets)
    target_pot = reduce_call(True)(term, weights_tgt, weights_tgt)
    source_pot = weights_src
    for sweep in range(ITERS):
        last = sweep == ITERS - 1
        source_pot, term = rows(sweep == 0, not last)(
            block_columns, block_counts, sources, weights_src, source_pot, target_pot, picked
        )
        if not last:
            target_pot = reduce_call(False)(term, weights_tgt, target_pot)
    return (source_pot.reshape(-1), term.reshape(-1))


def solution(mesh):
    return jax.shard_map(
        local,
        mesh=mesh,
        in_specs=(
            P(("groups", "row"), None),
            P("groups", None),
            P(("groups", "row")),
            P("groups"),
            P(("groups", "row"), None),
            P(("groups", "row")),
        ),
        out_specs=(P(("groups", "row")), P(("groups", "row"))),
        check_vma=False,
    )
```

```python
import functools

import jax
import jax.numpy as jnp
from jax import lax
from jax.experimental import pallas as pl
from jax.experimental.pallas import tpu as pltpu
from jax.sharding import PartitionSpec as P

BLOCK = 256
ITERS = 3
FLOOR = -1e30
SMALL = 1e-20
GROUP = 16
ROWS = 32
AHEAD = 2
CHUNKS = 1
EXTRA = 16
HALVES = (pl.ds(0, BLOCK // 2), pl.ds(BLOCK // 2, BLOCK // 2))
VMEM_BYTES = 50 * 1024 * 1024


def scores_of(source_ref, gathered, which, slot, slots):
    width = gathered.shape[1]
    source = source_ref[pl.ds(pl.multiple_of(which * BLOCK, BLOCK), BLOCK), pl.ds(0, width)]
    targets = gathered[which * slots + slot]
    return jnp.dot(source, targets, preferred_element_type=jnp.float32)


def pieces(x):
    high = x.astype(jnp.bfloat16).astype(jnp.float32)
    rest = x - high
    middle = rest.astype(jnp.bfloat16).astype(jnp.float32)
    return high, middle, rest - middle


def with_pieces(x, index, at, base):
    for k, piece in enumerate(pieces(x)):
        base = jnp.where(index == at + k, piece, base)
    return base


def fetch(columns_ref, targets_ref, gathered, sems, index):
    slots = columns_ref.shape[1]
    column = columns_ref[index // slots, lax.rem(index, slots)]
    return pltpu.make_async_copy(
        targets_ref.at[:, pl.ds(pl.multiple_of(column * BLOCK, BLOCK), BLOCK)],
        gathered.at[index],
        sems.at[index],
    )


def row_of(columns_ref, counts_ref, which, slot, target_count):
    return jnp.where(slot < counts_ref[which], columns_ref[which, slot], target_count)


def clear(ref, target_count, value):
    own = ref.shape[0]

    def one(i, _):
        rows = pl.ds(pl.multiple_of(i * ROWS, ROWS), ROWS)
        for p in range(own):
            ref[p, rows, :] = jnp.full((ROWS, BLOCK), value, jnp.float32)
        return 0

    lax.fori_loop(0, target_count // ROWS, one, 0)


def first_columns(
    columns_ref, counts_ref, source_ref, targets_ref, out_ref, gathered, tops, sums, sems
):
    own, slots = columns_ref.shape
    target_count = out_ref.shape[0]
    groups = own * slots // GROUP

    def start(group):
        for k in range(GROUP):
            fetch(columns_ref, targets_ref, gathered, sems, group * GROUP + k).start()

    for group in range(min(AHEAD, groups)):
        start(group)
    clear(tops, target_count, FLOOR)
    clear(sums, target_count, 0.0)

    def work(group):
        for k in range(GROUP):
            fetch(columns_ref, targets_ref, gathered, sems, group * GROUP + k).wait()
        which = group * GROUP // slots
        for k in range(GROUP):
            slot = lax.rem(group * GROUP, slots) + k
            row = row_of(columns_ref, counts_ref, which, slot, target_count)
            scores = scores_of(source_ref, gathered, which, slot, slots)
            top = jnp.max(scores, axis=0, keepdims=True)
            tops[which, pl.ds(row, 1), :] = top
            sums[which, pl.ds(row, 1), :] = jnp.sum(jnp.exp(scores - top), axis=0, keepdims=True)

    def ahead(group, _):
        start(group + AHEAD)
        work(group)
        return 0

    def rest(group, _):
        work(group)
        return 0

    full = max(groups - AHEAD, 0)
    lax.fori_loop(0, full, ahead, 0)
    lax.fori_loop(full, groups, rest, 0)

    def combine(i, _):
        rows = pl.ds(pl.multiple_of(i * ROWS, ROWS), ROWS)
        top = tops[0, rows, :]
        for p in range(1, own):
            top = jnp.maximum(top, tops[p, rows, :])
        total = jnp.zeros_like(top)
        for p in range(own):
            total = total + sums[p, rows, :] * jnp.exp(tops[p, rows, :] - top)
        used = total > 0.0
        out_ref[rows, :] = jnp.where(used, top + jnp.log(jnp.where(used, total, 1.0)), FLOOR)
        return 0

    lax.fori_loop(0, target_count // ROWS, combine, 0)


def halves(x):
    return x[:, : BLOCK // 2], x[:, BLOCK // 2 :]


def rows_kernel(
    first,
    columns_out,
    columns_ref,
    counts_ref,
    source_ref,
    weights_ref,
    old_ref,
    pot_ref,
    gathered,
    new_ref,
    *rest,
):
    if columns_out:
        out_ref, partial, source, shift, held, dense = rest
    else:
        own_ref, partial, source, shift = rest
    own, slots = columns_ref.shape
    target_count = pot_ref.shape[0]
    if columns_out:
        clear(dense, target_count, 0.0)
    else:
        share = own_ref.shape[0]
        mine = pl.multiple_of(lax.axis_index("row") * share, 8)
        own_ref[...] = pot_ref[pl.ds(mine, share), :]
    width = gathered.shape[1]
    extra_row = lax.broadcasted_iota(jnp.int32, (EXTRA, BLOCK), 0)
    ones = jnp.where(extra_row < 3, 1.0, 0.0)
    lane = lax.broadcasted_iota(jnp.int32, (BLOCK, width + EXTRA), 1)

    def one_source(which, _):
        own_rows = pl.ds(pl.multiple_of(which * BLOCK, BLOCK), BLOCK)
        groups = slots // GROUP

        def set_source(offset):
            base = source_ref[own_rows, :].astype(jnp.float32)
            source[...] = with_pieces(offset, lane, width, base).astype(source.dtype)

        def shifted(slot):
            column = columns_ref[which, slot]
            pot = pot_ref[pl.ds(column, 1), :] + jnp.where(slot < counts_ref[which], 0.0, FLOOR)
            extra = with_pieces(pot, extra_row, 3, ones).astype(source.dtype)
            targets = jnp.concatenate([gathered[which * slots + slot], extra], axis=0)
            return jnp.dot(source[...], targets, preferred_element_type=jnp.float32)

        def sum_group(i, _):
            total = partial[...]
            for k in range(GROUP):
                slot = i * GROUP + k
                terms = jnp.exp(shifted(slot))
                if columns_out:
                    held[slot] = terms
                low, high = halves(terms)
                total = total + (low + high)
            partial[...] = total
            return 0

        def sum_all(offset):
            shift[...] = offset
            set_source(offset)
            partial[...] = jnp.zeros(partial.shape, jnp.float32)
            lax.fori_loop(0, groups, sum_group, 0)

        if first:
            sum_all(jnp.zeros((BLOCK, 1), jnp.float32))

            @pl.when(jnp.min(jnp.sum(partial[...], axis=1, keepdims=True)) < SMALL)
            def _():
                set_source(jnp.zeros((BLOCK, 1), jnp.float32))
                partial[...] = jnp.full(partial.shape, FLOOR, jnp.float32)

                def top_group(i, _):
                    best = partial[...]
                    for k in range(GROUP):
                        low, high = halves(shifted(i * GROUP + k))
                        best = jnp.maximum(best, jnp.maximum(low, high))
                    partial[...] = best
                    return 0

                lax.fori_loop(0, groups, top_group, 0)
                sum_all(-jnp.max(partial[...], axis=1, keepdims=True))
        else:
            sum_all(old_ref[own_rows, :])
        offset = shift[...]
        total = jnp.sum(partial[...], axis=1, keepdims=True)
        weights = weights_ref[own_rows, :]
        new_ref[own_rows, :] = weights + offset - jnp.log(total)
        if columns_out:
            partial[...] = jnp.broadcast_to(jnp.exp(weights) / total, partial.shape)

            def column_group(i, _):
                factor = partial[...]
                for k in range(GROUP):
                    slot = i * GROUP + k
                    row = row_of(columns_ref, counts_ref, which, slot, target_count)
                    parts = [
                        jnp.sum(held[slot, :, lanes] * factor, axis=0, keepdims=True)
                        for lanes in HALVES
                    ]
                    dense[which, pl.ds(row, 1), :] = jnp.concatenate(parts, axis=1)
                return 0

            lax.fori_loop(0, groups, column_group, 0)
        return 0

    lax.fori_loop(0, own, one_source, 0)

    if columns_out:

        def combine(i, _):
            rows = pl.ds(pl.multiple_of(i * ROWS, ROWS), ROWS)
            total = dense[0, rows, :]
            for p in range(1, own):
                total = total + dense[p, rows, :]
            out_ref[rows, :] = total
            return 0

        lax.fori_loop(0, target_count // ROWS, combine, 0)


def stages_of(devices):
    if devices % 16 == 0:
        out = [(2, 1), (8, 2)]
        return out if devices == 16 else out + [(devices // 16, 16)]
    radices = []
    rest = devices
    if rest % 2 == 0:
        radices.append(2)
        rest //= 2
    while rest > 1:
        if rest % 4 == 0 and (rest & (rest - 1)) == 0 and rest.bit_length() % 2 == 1:
            radix = 4
        elif rest % 2 == 0:
            radix = 2
        else:
            radix = rest
        radices.append(radix)
        rest //= radix
    stages = []
    stride = 1
    for radix in radices:
        stages.append((radix, stride))
        stride *= radix
    return stages


def reduce_kernel(
    first,
    stages,
    term_ref,
    weights_ref,
    old_ref,
    out_ref,
    total,
    landed,
    weights_own,
    old_own,
    send_sems,
    recv_sems,
    local_sems,
):
    me = lax.axis_index("row")
    barrier = pltpu.get_barrier_semaphore()
    greeted = 0
    for radix, stride in stages:
        digit = lax.rem(me // stride, radix)
        for k in range(1, radix):
            peer = me + (lax.rem(digit + k, radix) - digit) * stride
            pl.semaphore_signal(
                barrier, inc=1, device_id={"row": peer}, device_id_type=pl.DeviceIdType.MESH
            )
            greeted += 1
    chunk = term_ref.shape[0] // CHUNKS
    share = chunk
    for radix, _ in stages:
        share //= radix
    orders = []
    bases = []
    for c in range(CHUNKS):
        rest = stages[1:]
        turn = c % len(rest) if rest else 0
        orders.append(stages[:1] + rest[turn:] + rest[:turn])
        base = c * chunk
        piece = chunk
        levels = [base]
        for radix, stride in orders[c]:
            piece //= radix
            base = base + lax.rem(me // stride, radix) * piece
            levels.append(base)
        bases.append(levels)
    local = []
    for c in range(CHUNKS):
        rows = pl.ds(pl.multiple_of(bases[c][-1], 8), share)
        near = pl.ds(c * share, share)
        sources = [(weights_ref, weights_own)] if first else [
            (weights_ref, weights_own), (old_ref, old_own)
        ]
        for source, target in sources:
            local.append(
                pltpu.make_async_copy(source.at[rows], target.at[near], local_sems.at[len(local)])
            )
    for copy in local:
        copy.start()
    pl.semaphore_wait(barrier, greeted)

    sent = []

    def send(source, start, target, target_start, size, peer):
        index = len(sent)
        copy = pltpu.make_async_remote_copy(
            src_ref=source.at[pl.ds(pl.multiple_of(start, 8), size)],
            dst_ref=target.at[pl.ds(pl.multiple_of(target_start, 8), size)],
            send_sem=send_sems.at[index],
            recv_sem=recv_sems.at[index],
            device_id={"row": peer},
            device_id_type=pl.DeviceIdType.MESH,
        )
        copy.start()
        sent.append(copy)
        return copy

    flying = [[] for _ in range(CHUNKS)]
    places = [0] * CHUNKS
    sizes = [chunk] * CHUNKS
    offset = 0

    def fold(c, number):
        radix, _ = orders[c][number]
        size = sizes[c]
        step = min(ROWS, size)
        mine = bases[c][number + 1]
        place = places[c]
        current = term_ref if number == 0 else total
        last = number == len(stages) - 1

        def one(i, _):
            rows = pl.ds(pl.multiple_of(mine + i * step, 8), step)
            parts = [current[rows, :]]
            for k in range(1, radix):
                start = pl.multiple_of(place + (k - 1) * size + i * step, 8)
                parts.append(landed[pl.ds(start, step), :])
            if first:
                top = functools.reduce(jnp.maximum, parts)
                value = top + jnp.log(sum(jnp.exp(part - top) for part in parts))
            else:
                value = sum(parts[1:], parts[0])
            if last:
                near = pl.ds(pl.multiple_of(c * share + i * step, 8), step)
                if first:
                    out_ref[rows, :] = weights_own[near, :] - value
                else:
                    out_ref[rows, :] = weights_own[near, :] + old_own[near, :] - jnp.log(value)
            else:
                total[rows, :] = value
            return 0

        lax.fori_loop(0, size // step, one, 0)

    for number in range(len(stages) + 1):
        if number == len(stages):
            for copy in local:
                copy.wait()
        for c in range(CHUNKS):
            for copy in flying[c]:
                copy.wait_recv()
            if number > 0:
                fold(c, number - 1)
            if number == len(stages):
                continue
            radix, stride = orders[c][number]
            digit = lax.rem(me // stride, radix)
            sizes[c] //= radix
            places[c] = offset
            flying[c] = []
            for k in range(1, radix):
                other = lax.rem(digit + k, radix)
                flying[c].append(
                    send(
                        term_ref if number == 0 else total,
                        bases[c][number] + other * sizes[c],
                        landed,
                        offset,
                        sizes[c],
                        me + (other - digit) * stride,
                    )
                )
                offset += sizes[c]

    flying = [[] for _ in range(CHUNKS)]
    for number in reversed(range(len(stages))):
        for c in range(CHUNKS):
            for copy in flying[c]:
                copy.wait_recv()
            radix, stride = orders[c][number]
            digit = lax.rem(me // stride, radix)
            start = bases[c][number + 1]
            flying[c] = []
            for k in range(1, radix):
                other = lax.rem(digit + k, radix)
                flying[c].append(
                    send(out_ref, start, out_ref, start, sizes[c], me + (other - digit) * stride)
                )
            sizes[c] *= radix
    for c in range(CHUNKS):
        for copy in flying[c]:
            copy.wait_recv()
    for copy in sent:
        copy.wait_send()


def local(
    source_features, target_features, source_weights, target_weights, block_columns, block_counts
):
    own, slots = block_columns.shape
    target_count = target_features.shape[0] // BLOCK
    width = target_features.shape[1]
    cells = source_features.shape[0]
    carriers = jnp.broadcast_to(
        jnp.where((jnp.arange(EXTRA) >= 3) & (jnp.arange(EXTRA) < 6), 1.0, 0.0), (cells, EXTRA)
    )
    sources = jnp.concatenate([source_features, carriers.astype(source_features.dtype)], axis=1)
    devices = lax.axis_size("row")
    stages = stages_of(devices)
    share = target_count // devices
    targets = target_features.T
    weights_tgt = target_weights.reshape(target_count, BLOCK)
    weights_src = source_weights.reshape(cells, 1)

    in_smem = pl.BlockSpec(memory_space=pltpu.SMEM)
    in_vmem = pl.BlockSpec(memory_space=pltpu.VMEM)
    anywhere = pl.BlockSpec(memory_space=pl.ANY)
    in_hbm = pl.BlockSpec(memory_space=pltpu.HBM)
    params = pltpu.CompilerParams(vmem_limit_bytes=VMEM_BYTES)
    gathered = jax.ShapeDtypeStruct((own * slots, width, BLOCK), source_features.dtype)
    fetches = pltpu.SemaphoreType.DMA((own * slots,))
    dense = pltpu.VMEM((own, target_count + 8, BLOCK), jnp.float32)
    whole = jax.ShapeDtypeStruct((target_count, BLOCK), jnp.float32)
    part = jax.ShapeDtypeStruct((share, BLOCK), jnp.float32)
    per_source = jax.ShapeDtypeStruct((cells, 1), jnp.float32)

    first_term = pl.pallas_call(
        first_columns,
        out_shape=(whole, gathered),
        in_specs=[in_smem, in_smem, in_vmem, in_hbm],
        out_specs=(in_vmem, in_vmem),
        scratch_shapes=[dense, dense, fetches],
        compiler_params=params,
        name="first_columns",
    )

    def rows(first, columns_out):
        partial = pltpu.VMEM((BLOCK, BLOCK // 2), jnp.float32)
        source = pltpu.VMEM((BLOCK, width + EXTRA), source_features.dtype)
        shift = pltpu.VMEM((BLOCK, 1), jnp.float32)
        held = pltpu.VMEM((slots, BLOCK, BLOCK), jnp.float32)
        return pl.pallas_call(
            functools.partial(rows_kernel, first, columns_out),
            out_shape=(per_source, whole if columns_out else part),
            in_specs=[in_smem, in_smem, in_vmem, in_vmem, in_vmem, in_vmem, in_vmem],
            out_specs=(in_vmem, in_vmem),
            scratch_shapes=[partial, source, shift] + ([held, dense] if columns_out else []),
            compiler_params=params,
            name="rows",
        )

    messages = 2 * CHUNKS * sum(radix - 1 for radix, _ in stages)

    def reduce_call(first):
        return pl.pallas_call(
            functools.partial(reduce_kernel, first, stages),
            out_shape=whole,
            in_specs=[in_vmem, anywhere, anywhere],
            out_specs=in_vmem,
            scratch_shapes=[
                pltpu.VMEM((target_count, BLOCK), jnp.float32),
                pltpu.VMEM((target_count, BLOCK), jnp.float32),
                pltpu.VMEM((share, BLOCK), jnp.float32),
                pltpu.VMEM((share, BLOCK), jnp.float32),
                pltpu.SemaphoreType.DMA((messages,)),
                pltpu.SemaphoreType.DMA((messages,)),
                pltpu.SemaphoreType.DMA((2 * CHUNKS,)),
            ],
            compiler_params=pltpu.CompilerParams(
                vmem_limit_bytes=VMEM_BYTES,
                collective_id=0 if first else 1,
                has_side_effects=True,
            ),
            name="reduce",
        )

    term, picked = first_term(block_columns, block_counts, sources, targets)
    target_pot = reduce_call(True)(term, weights_tgt, weights_tgt)
    source_pot = weights_src
    for sweep in range(ITERS):
        last = sweep == ITERS - 1
        source_pot, term = rows(sweep == 0, not last)(
            block_columns, block_counts, sources, weights_src, source_pot, target_pot, picked
        )
        if not last:
            target_pot = reduce_call(False)(term, weights_tgt, target_pot)
    return (source_pot.reshape(-1), term.reshape(-1))


def solution(mesh):
    return jax.shard_map(
        local,
        mesh=mesh,
        in_specs=(
            P(("groups", "row"), None),
            P("groups", None),
            P(("groups", "row")),
            P("groups"),
            P(("groups", "row"), None),
            P(("groups", "row")),
        ),
        out_specs=(P(("groups", "row")), P(("groups", "row"))),
        check_vma=False,
    )
```
